512 devices in a mesh: vocab: 16 (over y, core), docs: 32 (over x, z).
Axes of the slice: x: 4, y: 8, z: 8, core: 2. Of those that a mesh axis runs over, the one named last changes fastest.
Arguments:
- counts: bfloat16 [65536, 4, 128], P(('vocab', 'docs')), may hold values from 0 to 2
- doc_owner: int32 [65536, 4], P(('vocab', 'docs')), may hold values from 0 to 511, all different within a row; in each aligned block of 128 rows (0 to 127, 128 to 255, ...) at most 2 rows name the same one
- doc_sub: int32 [65536, 4], P(('vocab', 'docs')), may hold values from 0 to 7
- doc_len: int32 [65536], P(('vocab', 'docs')), may hold values from 256 to 1023
- first_weight: bfloat16 [524288, 2048], P(('vocab', 'docs')), may hold values from -0.25 to 0.25
- first_bias: float32 [2048], replicated, may hold values from -3 to 3
- head_weight: bfloat16 [2048, 1536], P('vocab', 'docs'), may hold values from -0.125 to 0.125
- head_bias: float32 [1536], replicated, may hold values from -4 to 4
- factor: bfloat16 [1536, 1536], P('vocab', 'docs'), as said below
- noise_draw: bfloat16 [65536, 1536], P(('vocab', 'docs')), may hold values from -5 to 5
Outputs:
- sample: bfloat16 [65536, 1536], P(('vocab', 'docs'))
The draws below stay inside these ranges and needn't reach their ends.
Inputs may be any that keep to these rules, and one draw needn't show every extreme that they name: `doc_owner`: each document names 4 different owners. The documents of one device name one owner in at most 2 slots, and on some device some owner is named in exactly 2 slots. `factor`: lower triangular; diagonal entries lie between 0.5 and 1.5.
All inputs are finite; a program needn't handle non-finite values.
Results may differ from the reference program's by a relative error of at most 0.0038.
Values may be sent and summed in bfloat16 or wider, within the bound.
No kernel may reach another device: no remote copies, remote signals or barrier semaphores. Data moves between devices by JAX's collectives and lax.ppermute only.
A program may use at most 128 MiB of HBM per device.

```python
import math
import jax
import jax.numpy as jnp
import numpy as np
from jax import lax

VOC_DEV = 1024
H = 2048
K = 1536
NB = 4
DOC_DEV = 128
VOCAB = 524288
NDOC = 65536
CAP = 2
DEVICES = 512


def draw_factor(key, part):
    key_diag = jax.random.fold_in(key, 11)
    key_low = jax.random.fold_in(key, 23)
    row_index = jnp.arange(K)[:, None]
    col_index = jnp.arange(K)[None, :]
    diagonal = jax.random.uniform(key_diag, (K, 1), jnp.float32, 0.5, 1.5)
    lower_vals = jax.random.normal(key_low, (K, K), jnp.float32)
    off_scale = 0.6 / jnp.sqrt(jnp.maximum(row_index, 1).astype(jnp.float32))
    lower_part = jnp.where(col_index < row_index, lower_vals * off_scale, 0.0)
    result = lower_part + jnp.where(col_index == row_index, diagonal, 0.0)
    return result.astype(jnp.bfloat16)


def touch_ends(entries, rng, least, top_value):
    longest = entries.shape.index(max(entries.shape))
    spots = []
    for shift in (0, 1):
        where = [jax.random.randint(jax.random.fold_in(rng, axis), (), 0, length) for axis, length in enumerate(entries.shape)]
        where[longest] = (where[longest] + shift) % entries.shape[longest]
        spots.append(tuple(where))
    return entries.at[spots[0]].set(least).at[spots[1]].set(top_value)


def steps_of(own_key, shape, shards, low, top_value):
    gain, own = 1.0, jax.random.fold_in(own_key, 6)
    for dim, parts in shards:
        steps = jnp.exp(jax.random.uniform(jax.random.fold_in(own, dim), (parts,), jnp.float32, low / len(shards), top_value / len(shards)))
        gain = gain * jnp.repeat(steps, shape[dim] // parts).reshape([-1 if axis == dim else 1 for axis in range(len(shape))])
    return gain


def assign_block(key, own, number, rows, amount, top, bound, lean):
    order = jax.random.permutation(key, amount)
    packed, ordinary = shares(amount, rows * top, bound, lean, True), shares(amount, rows * top, bound, lean, False)
    places = jnp.arange(amount)

    def named(sizes, turn):
        used = int((sizes > 0).sum())
        fixed = max(1, used // 4)
        shifted = fixed + (places - fixed + turn * (used - fixed)) % max(1, amount - fixed)
        return jnp.zeros((amount,), jnp.int32).at[order[jnp.where(places < fixed, places, shifted)]].set(jnp.asarray(sizes, jnp.int32))

    sizes = jnp.where(number % 4 == 0, named(packed, number // 4), named(ordinary, number - number // 4 - 1))
    mixed = jax.random.permutation(jax.random.fold_in(own, 3), amount)
    source_of, receiver = mixed[0:amount // 2 * 2:2], mixed[1:amount // 2 * 2:2]
    slack = jnp.minimum(sizes[source_of] - 1, bound - sizes[receiver]) // 2
    slack = jnp.where((source_of == order[0]) | (receiver == order[0]) | (sizes[receiver] == 0), 0, jnp.maximum(slack, 0))
    shifted = jax.random.randint(jax.random.fold_in(own, 4), (amount // 2,), 0, 1 << 20) % (slack + 1)
    sizes = sizes.at[source_of].add(-shifted).at[receiver].add(shifted)
    labels = jnp.searchsorted(jnp.cumsum(sizes), jnp.arange(rows * top), side="right").astype(jnp.int32)
    table = labels.reshape(top, rows).T
    table = table[jax.random.permutation(jax.random.fold_in(own, 1), rows)]
    turn = jax.random.randint(jax.random.fold_in(own, 2), (rows, 1), 0, top)
    return jnp.take_along_axis(table, (jnp.arange(top)[None, :] + turn) % top, axis=1)


def shares(count, total, limit, lean, full):
    weights = [(1 << 20) // math.isqrt(grade ** lean) + 1 for grade in range(1, count + 1)]
    largest = limit if full else min(limit, max(-(-total // count), total * weights[0] // sum(weights)))
    least = 1 if total - largest >= count - 1 else 0
    given, rest = [largest] + [least] * (count - 1), total - largest - least * (count - 1)
    while rest > 0:
        free = [i for i in range(1, count) if given[i] < largest] or [i for i in range(1, count) if given[i] < limit]
        mass, budget = sum([weights[i] for i in free]), rest
        for i in free:
            extra = min(limit - given[i], max(1, budget * weights[i] // mass), rest)
            given[i] = given[i] + extra
            rest = rest - extra
    return np.array(given)


def noise(rng, shape, deviation, bound, split=(), held_as=jnp.bfloat16):
    factor_of = steps_of(rng, shape, split, -0.22, 0.18) if split else 1.0
    entries = jax.random.normal(rng, shape, jnp.float32) * deviation * factor_of
    return jnp.minimum(jnp.maximum(entries, -bound), bound).astype(held_as)


def setup_inputs(seed: int = 0) -> dict:
    streams_of = jax.random.split(jax.random.key(seed), 11)
    counts = jnp.clip(2.0 * jax.random.uniform(streams_of[0], (NDOC, NB, 128), jnp.float32) ** steps_of(streams_of[0], (NDOC, NB, 128), ((0, 512),), -0.2, 0.2), 0.0, 2.0).astype(jnp.bfloat16)
    doc_owner_keys = jax.random.split(jax.random.fold_in(streams_of[1], 1), NDOC // DOC_DEV)
    doc_owner_turns = jax.random.permutation(jax.random.fold_in(streams_of[1], 3), NDOC // DOC_DEV)
    doc_owner = jax.vmap(lambda own, number: assign_block(jax.random.fold_in(streams_of[1], 2), own, number, DOC_DEV, DEVICES, NB, CAP, 2))(doc_owner_keys, doc_owner_turns).reshape((NDOC, NB))
    doc_sub = touch_ends(jax.random.randint(streams_of[2], (NDOC, NB), 0, VOC_DEV // 128), jax.random.fold_in(streams_of[2], 1), 0, (VOC_DEV // 128) - 1).astype(jnp.int32)
    doc_len = touch_ends(jax.random.randint(streams_of[3], (NDOC,), 64 * NB, 256 * NB), jax.random.fold_in(streams_of[3], 1), 64 * NB, (256 * NB) - 1).astype(jnp.int32)
    first_weight = noise(streams_of[4], (VOCAB, H), (128 * NB) ** -0.5, 0.25, ((0, 512),))
    first_bias = noise(streams_of[5], (H,), 0.5, 3.0, (), jnp.float32)
    head_weight = noise(streams_of[6], (H, K), H ** -0.5, 0.125, ((0, 16), (1, 32)))
    head_bias = noise(streams_of[7], (K,), 1.0, 4.0, (), jnp.float32)
    factor = draw_factor(jax.random.fold_in(streams_of[10], 71), 0)
    noise_draw = noise(streams_of[9], (NDOC, K), 1.0, 5.0, ((0, 512),))
    return dict(counts=counts, doc_owner=doc_owner, doc_sub=doc_sub, doc_len=doc_len, first_weight=first_weight, first_bias=first_bias, head_weight=head_weight, head_bias=head_bias, factor=factor, noise_draw=noise_draw)


def reference(counts, doc_owner, doc_sub, doc_len, first_weight, first_bias, head_weight, head_bias, factor, noise_draw):
    per_owner = VOC_DEV // 128
    window = DEVICES * CAP
    owner_flat = doc_owner.reshape(-1).astype(jnp.int32)
    sub_flat = doc_sub.reshape(-1).astype(jnp.int32)
    doc_flat = jnp.repeat(jnp.arange(NDOC, dtype=jnp.int32), NB)
    flat_rows = counts.reshape(-1, 128)
    row_order = jnp.argsort(owner_flat, stable=True)
    sorted_owner = owner_flat[row_order]
    starts = jnp.searchsorted(sorted_owner, jnp.arange(DEVICES, dtype=jnp.int32), side="left").astype(jnp.int32)
    padded_rows = jnp.concatenate([flat_rows[row_order], jnp.zeros((window, 128), counts.dtype)], axis=0)
    padded_sub = jnp.concatenate([sub_flat[row_order], jnp.zeros((window,), jnp.int32)], axis=0)
    padded_doc = jnp.concatenate([doc_flat[row_order], jnp.full((window,), NDOC, jnp.int32)], axis=0)
    padded_owner = jnp.concatenate([sorted_owner, jnp.full((window,), -1, jnp.int32)], axis=0)
    weight_blocks = first_weight.reshape(DEVICES, VOC_DEV, H)

    def owner_step(summed, owner_index):
        row_begin = starts[owner_index]
        rows_here = lax.dynamic_slice_in_dim(padded_rows, row_begin, window, 0)
        sub_here = lax.dynamic_slice_in_dim(padded_sub, row_begin, window, 0)
        doc_here = lax.dynamic_slice_in_dim(padded_doc, row_begin, window, 0)
        owner_here = lax.dynamic_slice_in_dim(padded_owner, row_begin, window, 0)
        row_valid = owner_here == owner_index
        select = ((sub_here[:, None] == jnp.arange(per_owner, dtype=jnp.int32)[None, :]) & row_valid[:, None]).astype(jnp.bfloat16)
        spread = (select[:, :, None] * rows_here[:, None, :]).reshape(window, per_owner * 128)
        owner_terms = jnp.dot(spread, weight_blocks[owner_index], preferred_element_type=jnp.float32).astype(jnp.bfloat16)
        doc_target = jnp.where(row_valid, doc_here, NDOC)
        summed = summed.at[doc_target].add(owner_terms.astype(jnp.float32), mode="drop")
        return summed, owner_index

    summed = lax.scan(owner_step, jnp.zeros((NDOC, H), jnp.float32), jnp.arange(DEVICES, dtype=jnp.int32))[0]
    length_scale = (128.0 * NB) / doc_len.astype(jnp.float32)
    hidden = jax.nn.softplus(summed * length_scale[:, None] + first_bias).astype(jnp.bfloat16)
    location = jnp.dot(hidden, head_weight, preferred_element_type=jnp.float32) + head_bias
    correlated = lax.dot_general(noise_draw, factor, (((1,), (1,)), ((), ())), preferred_element_type=jnp.float32)
    return (location + correlated).astype(jnp.bfloat16)
```

```python
import functools

import jax
import jax.numpy as jnp
from jax import lax
from jax.experimental import pallas as pl
from jax.experimental.pallas import tpu as pltpu
from jax.sharding import PartitionSpec as P

AXES = ("vocab", "docs")
VMEM = pl.BlockSpec(memory_space=pltpu.VMEM)
SMEM = pl.BlockSpec(memory_space=pltpu.SMEM)
LANES = 128
PARAMS = pltpu.CompilerParams(vmem_limit_bytes=56 * 1024 * 1024)
NT = (((1,), (1,)), ((), ()))


def route_kernel(owner_ref, sub_ref, rows_ref, send_ref, place_ref):
    slots = owner_ref.shape[1]
    devices = send_ref.shape[0]
    owner = owner_ref[...]
    named = owner == lax.broadcasted_iota(jnp.int32, (devices, slots), 0)
    named_b = jnp.where(named, 1.0, 0.0).astype(jnp.bfloat16)
    earlier = lax.broadcasted_iota(jnp.int32, (slots, slots), 0) < lax.broadcasted_iota(
        jnp.int32, (slots, slots), 1
    )
    before = jnp.dot(
        named_b,
        jnp.where(earlier, 1.0, 0.0).astype(jnp.bfloat16),
        preferred_element_type=jnp.float32,
    )
    second = jnp.where(named & (before > 0.5), 1.0, 0.0)
    position = jnp.max(second, axis=0, keepdims=True)
    place_ref[...] = owner * 2 + position.astype(jnp.int32)
    rows = rows_ref[...]
    sub = jnp.broadcast_to(sub_ref[...].astype(jnp.float32), (LANES, slots)).astype(jnp.bfloat16)
    picks = (jnp.where(named & (before < 0.5), 1.0, 0.0).astype(jnp.bfloat16), second.astype(jnp.bfloat16))
    for p, pick in enumerate(picks):
        send_ref[:, p * LANES : (p + 1) * LANES] = jnp.dot(
            pick, rows, preferred_element_type=jnp.float32
        ).astype(jnp.bfloat16)
        send_ref[:, (2 + p) * LANES : (3 + p) * LANES] = lax.dot_general(
            pick, sub, NT, preferred_element_type=jnp.float32
        ).astype(jnp.bfloat16)


def owner_kernel(got_ref, weight_ref, out_ref, spread, stage):
    devices = got_ref.shape[0]
    blocks = weight_ref.shape[0] // LANES
    hidden_width = weight_ref.shape[1]
    for p in range(2):
        rows = got_ref[:, p * LANES : (p + 1) * LANES]
        sub = got_ref[:, (2 + p) * LANES : (3 + p) * LANES].astype(jnp.float32)
        for b in range(blocks):
            spread[p * devices : (p + 1) * devices, b * LANES : (b + 1) * LANES] = jnp.where(
                sub == float(b), rows.astype(jnp.float32), 0.0
            ).astype(jnp.bfloat16)
    width = 256
    parts = hidden_width // LANES
    for g in range(parts // 8):
        for cc in range(8 * LANES // width):
            column = g * 8 * LANES + cc * width
            terms = jnp.dot(
                spread[...], weight_ref[:, column : column + width], preferred_element_type=jnp.float32
            )
            for p in range(2):
                for k in range(width // LANES):
                    c = cc * (width // LANES) + k
                    stage[p, pl.ds(c, devices, stride=8), :] = terms[
                        p * devices : (p + 1) * devices, k * LANES : (k + 1) * LANES
                    ]
        for p in range(2):
            out_ref[:, p * parts + 8 * g : p * parts + 8 * g + 8, :] = (
                stage[p].reshape(devices, 8, LANES).astype(jnp.bfloat16)
            )


def finish_kernel(place_ref, got_ref, scale_ref, bias_ref, head_ref, extra_ref, out_ref, total, head, sem):
    docs, topics = out_ref.shape
    parts = got_ref.shape[1]
    copy = pltpu.make_async_copy(head_ref.at[:, :, pl.ds(0, LANES)], head, sem)
    copy.start()

    @pl.loop(0, docs, unroll=4)
    def _(n):
        value = got_ref[place_ref[0, n]].astype(jnp.float32)
        for slot in range(1, 4):
            value += got_ref[place_ref[0, slot * docs + n]].astype(jnp.float32)
        total[pl.ds(n * parts, parts), :] = value

    copy.wait()
    scale = scale_ref[...]
    result = extra_ref[...]
    for c in range(0, parts, 2):
        pair, columns = [], []
        for k in (c, c + 1):
            v = total[pl.ds(k, docs, stride=parts), :] * scale + bias_ref[:, k * LANES : (k + 1) * LANES]
            pair.append(jnp.maximum(v, 0.0) + jnp.log1p(jnp.exp(-jnp.abs(v))))
            columns.append(head[k])
        hidden = jnp.concatenate(pair, axis=1).astype(jnp.bfloat16)
        result += lax.dot_general(
            hidden, jnp.concatenate(columns, axis=1), NT, preferred_element_type=jnp.float32
        )
    out_ref[...] = result.astype(jnp.bfloat16)


def local(
    counts,
    doc_owner,
    doc_sub,
    doc_len,
    first_weight,
    first_bias,
    head_weight,
    head_bias,
    factor,
    noise_draw,
):
    vocab_devices = lax.axis_size("vocab")
    docs_devices = lax.axis_size("docs")
    devices = vocab_devices * docs_devices
    docs_here, slot_count, block_width = counts.shape
    slots = docs_here * slot_count
    hidden_width = first_weight.shape[1]
    parts = hidden_width // LANES
    topics = noise_draw.shape[1]
    topic_cols = head_weight.shape[1]
    factor_rows = factor.shape[0]

    panel = jnp.concatenate(
        [head_weight.T, jnp.pad(factor.T, ((0, 0), (0, LANES - factor_rows)))], axis=1
    )
    panels = lax.all_gather(panel, AXES, axis=0, tiled=True)
    panels = panels.reshape(vocab_devices, docs_devices * topic_cols, 2 * LANES)

    rows = counts.transpose(1, 0, 2).reshape(slots, block_width)
    owner_flat = doc_owner.T.reshape(1, slots)
    sub_flat = doc_sub.T.reshape(1, slots)
    send, place = pl.pallas_call(
        route_kernel,
        out_shape=(
            jax.ShapeDtypeStruct((devices, 4 * LANES), jnp.bfloat16),
            jax.ShapeDtypeStruct((1, slots), jnp.int32),
        ),
        in_specs=[VMEM] * 3,
        out_specs=(VMEM, VMEM),
        compiler_params=PARAMS,
        cost_estimate=pl.CostEstimate(flops=10**9, bytes_accessed=10**6, transcendentals=0),
    )(owner_flat, sub_flat, rows)
    got = lax.all_to_all(
        send.reshape(devices, 4, LANES), AXES, split_axis=0, concat_axis=0, tiled=True
    )
    terms = pl.pallas_call(
        owner_kernel,
        out_shape=jax.ShapeDtypeStruct((devices, 2 * parts, LANES), jnp.bfloat16),
        in_specs=[VMEM] * 2,
        out_specs=VMEM,
        scratch_shapes=[
            pltpu.VMEM((2 * devices, first_weight.shape[0]), jnp.bfloat16),
            pltpu.VMEM((2, devices * 8, LANES), jnp.float32),
        ],
        compiler_params=PARAMS,
        cost_estimate=pl.CostEstimate(flops=5 * 10**9, bytes_accessed=10**7, transcendentals=0),
    )(got.reshape(devices, 4 * LANES), first_weight)
    returned = lax.all_to_all(terms, AXES, split_axis=0, concat_axis=0, tiled=True)
    returned = returned.reshape(2 * devices, parts, LANES)

    correlated = jnp.einsum(
        "nj,vjk->nvk",
        noise_draw,
        panels[:, :, LANES : LANES + factor_rows],
        preferred_element_type=jnp.float32,
    ).reshape(docs_here, topics)
    extra = correlated + head_bias
    scale = (128.0 * slot_count / doc_len.astype(jnp.float32))[:, None]
    return pl.pallas_call(
        finish_kernel,
        out_shape=jax.ShapeDtypeStruct((docs_here, topics), jnp.bfloat16),
        in_specs=[SMEM, VMEM, VMEM, VMEM, pl.BlockSpec(memory_space=pl.ANY), VMEM],
        out_specs=VMEM,
        scratch_shapes=[
            pltpu.VMEM((docs_here * parts, LANES), jnp.float32),
            pltpu.VMEM((vocab_devices, topics, LANES), jnp.bfloat16),
            pltpu.SemaphoreType.DMA,
        ],
        compiler_params=PARAMS,
        cost_estimate=pl.CostEstimate(flops=10**9, bytes_accessed=10**7, transcendentals=10**6),
    )(place, returned, scale, first_bias.reshape(1, hidden_width), panels, extra)


def solution(mesh):
    return jax.shard_map(
        local,
        mesh=mesh,
        in_specs=(
            P(("vocab", "docs"), None, None),
            P(("vocab", "docs"), None),
            P(("vocab", "docs"), None),
            P(("vocab", "docs")),
            P(("vocab", "docs"), None),
            P(),
            P("vocab", "docs"),
            P(),
            P("vocab", "docs"),
            P(("vocab", "docs"), None),
        ),
        out_specs=P(("vocab", "docs"), None),
        check_vma=False,
    )
```

```python
import jax
import jax.numpy as jnp
from jax import lax
from jax.experimental import pallas as pl
from jax.experimental.pallas import tpu as pltpu
from jax.sharding import PartitionSpec as P

AXES = ("y", "core", "x", "z")
VMEM = pl.BlockSpec(memory_space=pltpu.VMEM)
SMEM = pl.BlockSpec(memory_space=pltpu.SMEM)
LANES = 128
PARAMS = pltpu.CompilerParams(vmem_limit_bytes=56 * 1024 * 1024)
NT = (((1,), (1,)), ((), ()))


def route_kernel(owner_ref, sub_ref, rows_ref, send_ref, place_ref):
    slots = owner_ref.shape[1]
    devices = send_ref.shape[0]
    owner = owner_ref[...]
    named = owner == lax.broadcasted_iota(jnp.int32, (devices, slots), 0)
    named_b = jnp.where(named, 1.0, 0.0).astype(jnp.bfloat16)
    earlier = lax.broadcasted_iota(jnp.int32, (slots, slots), 0) < lax.broadcasted_iota(
        jnp.int32, (slots, slots), 1
    )
    before = jnp.dot(
        named_b,
        jnp.where(earlier, 1.0, 0.0).astype(jnp.bfloat16),
        preferred_element_type=jnp.float32,
    )
    second = jnp.where(named & (before > 0.5), 1.0, 0.0)
    position = jnp.max(second, axis=0, keepdims=True)
    place_ref[...] = owner * 2 + position.astype(jnp.int32)
    rows = rows_ref[...]
    sub = jnp.broadcast_to(sub_ref[...].astype(jnp.float32), (LANES, slots)).astype(jnp.bfloat16)
    picks = (jnp.where(named & (before < 0.5), 1.0, 0.0).astype(jnp.bfloat16), second.astype(jnp.bfloat16))
    for p, pick in enumerate(picks):
        send_ref[:, p * LANES : (p + 1) * LANES] = jnp.dot(
            pick, rows, preferred_element_type=jnp.float32
        ).astype(jnp.bfloat16)
        send_ref[:, (2 + p) * LANES : (3 + p) * LANES] = lax.dot_general(
            pick, sub, NT, preferred_element_type=jnp.float32
        ).astype(jnp.bfloat16)


def owner_kernel(got_ref, weight_ref, out_ref, spread, stage):
    devices = got_ref.shape[0]
    blocks = weight_ref.shape[0] // LANES
    parts = weight_ref.shape[1] // LANES
    for p in range(2):
        rows = got_ref[:, p * LANES : (p + 1) * LANES]
        sub = got_ref[:, (2 + p) * LANES : (3 + p) * LANES].astype(jnp.float32)
        for b in range(blocks):
            spread[p * devices : (p + 1) * devices, b * LANES : (b + 1) * LANES] = jnp.where(
                sub == float(b), rows.astype(jnp.float32), 0.0
            ).astype(jnp.bfloat16)
    width = 256
    for g in range(parts // 8):
        for cc in range(8 * LANES // width):
            column = g * 8 * LANES + cc * width
            terms = jnp.dot(
                spread[...], weight_ref[:, column : column + width], preferred_element_type=jnp.float32
            )
            for p in range(2):
                for k in range(width // LANES):
                    c = cc * (width // LANES) + k
                    stage[p, pl.ds(c, devices, stride=8), :] = terms[
                        p * devices : (p + 1) * devices, k * LANES : (k + 1) * LANES
                    ]
        for p in range(2):
            out_ref[:, p * parts + 8 * g : p * parts + 8 * g + 8, :] = (
                stage[p].reshape(devices, 8, LANES).astype(jnp.bfloat16)
            )


def place_panels(shift_ref, panels_ref, lane, target, sem):
    z_devices, x_devices, rows = panels_ref.shape[1], panels_ref.shape[2], panels_ref.shape[3]
    copies = []
    for z in range(z_devices):
        for k in range(x_devices):
            x = lax.rem(shift_ref[0] + k, x_devices)
            begin = pl.multiple_of((x * z_devices + z) * rows, 16)
            copies.append(
                pltpu.make_async_copy(
                    panels_ref.at[:, z, k, :, pl.ds(lane, LANES)],
                    target.at[:, pl.ds(begin, rows), :],
                    sem.at[z * x_devices + k],
                )
            )
    for copy in copies:
        copy.start()
    return copies


def hidden_kernel(place_ref, got_ref, scale_ref, bias_ref, out_ref, total):
    docs = out_ref.shape[0]
    parts = got_ref.shape[1]

    @pl.loop(0, docs, unroll=4)
    def _(n):
        value = None
        for slot in range(4):
            row = got_ref[place_ref[0, slot * docs + n]].astype(jnp.float32)
            value = row if value is None else value + row
        total[pl.ds(pl.multiple_of(n * parts, parts), parts), :] = value

    scale = scale_ref[...]
    for c in range(parts):
        lanes = slice(c * LANES, (c + 1) * LANES)
        v = total[pl.ds(c, docs, stride=parts), :] * scale + bias_ref[:, lanes]
        soft = jnp.maximum(v, 0.0) + jnp.log1p(jnp.exp(-jnp.abs(v)))
        out_ref[:, lanes] = soft.astype(jnp.bfloat16)


def output_kernel(shift_ref, hidden_ref, noise_ref, panels_ref, bias_ref, out_ref, head, factor, head_sem, factor_sem):
    head_copies = place_panels(shift_ref, panels_ref, 0, head, head_sem)
    factor_copies = place_panels(shift_ref, panels_ref, LANES, factor, factor_sem)
    pieces = head.shape[0]
    width = out_ref.shape[1] // pieces
    for copy in head_copies:
        copy.wait()
    result = bias_ref[...]
    for v in range(0, pieces, 2):
        hidden = hidden_ref[:, v * LANES : (v + 2) * LANES]
        pair = jnp.concatenate([head[v], head[v + 1]], axis=1)
        result = result + lax.dot_general(hidden, pair, NT, preferred_element_type=jnp.float32)
    for copy in factor_copies:
        copy.wait()
    noise = noise_ref[...]
    parts = []
    for v in range(0, pieces, 2):
        pair = jnp.concatenate([factor[v], factor[v + 1]], axis=1)
        both = jnp.dot(noise, pair, preferred_element_type=jnp.float32)
        parts += [both[:, :width], both[:, LANES : LANES + width]]
    out_ref[...] = (result + jnp.concatenate(parts, axis=1)).astype(out_ref.dtype)


def local(
    counts,
    doc_owner,
    doc_sub,
    doc_len,
    first_weight,
    first_bias,
    head_weight,
    head_bias,
    factor,
    noise_draw,
):
    vocab_devices = lax.axis_size("y") * lax.axis_size("core")
    x_devices, z_devices = lax.axis_size("x"), lax.axis_size("z")
    docs_devices = x_devices * z_devices
    devices = vocab_devices * docs_devices
    docs_here, slot_count, block_width = counts.shape
    slots = docs_here * slot_count
    hidden_width = first_weight.shape[1]
    parts = hidden_width // LANES
    topics = noise_draw.shape[1]
    topic_cols = head_weight.shape[1]
    factor_rows = factor.shape[0]

    panel = jnp.concatenate(
        [head_weight.T, jnp.pad(factor.T, ((0, 0), (0, LANES - factor_rows)))], axis=1
    )
    line = [panel]
    for k in range(1, x_devices):
        line.append(lax.ppermute(panel, "x", [((i + k) % x_devices, i) for i in range(x_devices)]))
    rows = counts.transpose(1, 0, 2).reshape(slots, block_width)
    owner_flat = doc_owner.T.reshape(1, slots)
    sub_flat = doc_sub.T.reshape(1, slots)
    send, place = pl.pallas_call(
        route_kernel,
        out_shape=(
            jax.ShapeDtypeStruct((devices, 4 * LANES), jnp.bfloat16),
            jax.ShapeDtypeStruct((1, slots), jnp.int32),
        ),
        in_specs=[VMEM] * 3,
        out_specs=(VMEM, VMEM),
        compiler_params=PARAMS,
        cost_estimate=pl.CostEstimate(flops=10**9, bytes_accessed=10**6, transcendentals=0),
    )(owner_flat, sub_flat, rows)
    line, send = lax.optimization_barrier((line, send))
    panels = lax.all_gather(jnp.concatenate(line, axis=0), ("y", "core", "z"), axis=0, tiled=True)
    panels = panels.reshape(vocab_devices, z_devices, x_devices, topic_cols, 2 * LANES)
    shift = lax.axis_index("x").astype(jnp.int32).reshape(1)

    got = lax.all_to_all(
        send.reshape(devices, 4, LANES), AXES, split_axis=0, concat_axis=0, tiled=True
    )
    got = got.reshape(devices, 4 * LANES)
    terms = pl.pallas_call(
        owner_kernel,
        out_shape=jax.ShapeDtypeStruct((devices, 2 * parts, LANES), jnp.bfloat16),
        in_specs=[VMEM] * 2,
        out_specs=VMEM,
        scratch_shapes=[
            pltpu.VMEM((2 * devices, first_weight.shape[0]), jnp.bfloat16),
            pltpu.VMEM((2, devices * 8, LANES), jnp.float32),
        ],
        compiler_params=PARAMS,
        cost_estimate=pl.CostEstimate(flops=5 * 10**9, bytes_accessed=10**7, transcendentals=0),
    )(got, first_weight)
    returned = lax.all_to_all(terms, AXES, split_axis=0, concat_axis=0, tiled=True)
    returned = returned.reshape(2 * devices, parts, LANES)

    scale = (128.0 * slot_count / doc_len.astype(jnp.float32))[:, None]
    hidden = pl.pallas_call(
        hidden_kernel,
        out_shape=jax.ShapeDtypeStruct((docs_here, hidden_width), jnp.bfloat16),
        in_specs=[SMEM, VMEM, VMEM, VMEM],
        out_specs=VMEM,
        scratch_shapes=[pltpu.VMEM((docs_here * parts, LANES), jnp.float32)],
        compiler_params=PARAMS,
        cost_estimate=pl.CostEstimate(flops=10**7, bytes_accessed=10**7, transcendentals=10**6),
    )(place, returned, scale, first_bias.reshape(1, hidden_width))
    return pl.pallas_call(
        output_kernel,
        out_shape=jax.ShapeDtypeStruct((docs_here, topics), jnp.bfloat16),
        in_specs=[SMEM, VMEM, VMEM, pl.BlockSpec(memory_space=pl.ANY), VMEM],
        out_specs=VMEM,
        scratch_shapes=[
            pltpu.VMEM((vocab_devices, topics, LANES), jnp.bfloat16),
            pltpu.VMEM((vocab_devices, topics, LANES), jnp.bfloat16),
            pltpu.SemaphoreType.DMA((docs_devices,)),
            pltpu.SemaphoreType.DMA((docs_devices,)),
        ],
        compiler_params=PARAMS,
        cost_estimate=pl.CostEstimate(flops=10**9, bytes_accessed=10**7, transcendentals=0),
    )(shift, hidden, noise_draw, panels, head_bias.reshape(1, topics))


def solution(mesh):
    sizes = (8, 2, 4, 8)
    fine = jax.sharding.Mesh(mesh.devices.reshape(sizes), AXES)
    rows, vocab, docs = P(AXES), ("y", "core"), ("x", "z")
    return jax.shard_map(
        local,
        mesh=fine,
        in_specs=(rows, rows, rows, rows, rows, P(), P(vocab, docs), P(), P(vocab, docs), rows),
        out_specs=rows,
        check_vma=False,
    )
```

```python
import jax
import jax.numpy as jnp
from jax import lax
from jax.experimental import pallas as pl
from jax.experimental.pallas import tpu as pltpu
from jax.sharding import PartitionSpec as P

AXES = ("y", "core", "x", "z")
VMEM = pl.BlockSpec(memory_space=pltpu.VMEM)
SMEM = pl.BlockSpec(memory_space=pltpu.SMEM)
LANES = 128
PARAMS = pltpu.CompilerParams(vmem_limit_bytes=56 * 1024 * 1024)
NT = (((1,), (1,)), ((), ()))


def route_kernel(owner_ref, sub_ref, rows_ref, send_ref, place_ref, stage):
    slots = owner_ref.shape[1]
    devices = send_ref.shape[0] // 4
    owner = owner_ref[...]
    named = owner == lax.broadcasted_iota(jnp.int32, (devices, slots), 0)
    named_b = jnp.where(named, 1.0, 0.0).astype(jnp.bfloat16)
    earlier = lax.broadcasted_iota(jnp.int32, (slots, slots), 0) < lax.broadcasted_iota(
        jnp.int32, (slots, slots), 1
    )
    before = jnp.dot(
        named_b,
        jnp.where(earlier, 1.0, 0.0).astype(jnp.bfloat16),
        preferred_element_type=jnp.float32,
    )
    second = jnp.where(named & (before > 0.5), 1.0, 0.0)
    position = jnp.max(second, axis=0, keepdims=True)
    place_ref[...] = owner * 2 + position.astype(jnp.int32)
    rows = rows_ref[...]
    sub = jnp.broadcast_to(sub_ref[...].astype(jnp.float32), (LANES, slots)).astype(jnp.bfloat16)
    picks = (jnp.where(named & (before < 0.5), 1.0, 0.0).astype(jnp.bfloat16), second.astype(jnp.bfloat16))
    for p, pick in enumerate(picks):
        stage[pl.ds(p, devices, stride=4), :] = jnp.dot(
            pick, rows, preferred_element_type=jnp.float32
        )
        stage[pl.ds(2 + p, devices, stride=4), :] = lax.dot_general(
            pick, sub, NT, preferred_element_type=jnp.float32
        )
    send_ref[...] = stage[...].astype(jnp.bfloat16)


def owner_kernel(got_ref, weight_hbm, out_ref, spread, stage, rows_stage, weight_ref, sem):
    width = 256
    copies = [
        pltpu.make_async_copy(
            weight_hbm.at[:, pl.ds(k * width, width)],
            weight_ref.at[:, pl.ds(k * width, width)],
            sem.at[k],
        )
        for k in range(weight_ref.shape[1] // width)
    ]
    for copy in copies:
        copy.start()
    devices = got_ref.shape[0] // 4
    blocks = weight_ref.shape[0] // LANES
    rows_stage[...] = got_ref[...].astype(jnp.float32)
    parts = weight_ref.shape[1] // LANES
    for p in range(2):
        rows = rows_stage[pl.ds(p, devices, stride=4), :]
        sub = rows_stage[pl.ds(2 + p, devices, stride=4), :]
        for b in range(blocks):
            spread[p * devices : (p + 1) * devices, b * LANES : (b + 1) * LANES] = jnp.where(
                sub == float(b), rows, 0.0
            ).astype(jnp.bfloat16)
    for g in range(parts // 8):
        for cc in range(8 * LANES // width):
            column = g * 8 * LANES + cc * width
            copies[column // width].wait()
            terms = jnp.dot(
                spread[...], weight_ref[:, column : column + width], preferred_element_type=jnp.float32
            )
            for p in range(2):
                for k in range(width // LANES):
                    c = cc * (width // LANES) + k
                    stage[p, pl.ds(c, devices, stride=8), :] = terms[
                        p * devices : (p + 1) * devices, k * LANES : (k + 1) * LANES
                    ]
        for p in range(2):
            out_ref[:, p * parts + 8 * g : p * parts + 8 * g + 8, :] = (
                stage[p].reshape(devices, 8, LANES).astype(jnp.bfloat16)
            )


def place_panels(shift_ref, panels_ref, lane, target, sem):
    z_devices, x_devices, rows = panels_ref.shape[1], panels_ref.shape[2], panels_ref.shape[3]
    copies = []
    for z in range(z_devices):
        for k in range(x_devices):
            x = lax.rem(shift_ref[0] + k, x_devices)
            begin = pl.multiple_of((x * z_devices + z) * rows, 16)
            copies.append(
                pltpu.make_async_copy(
                    panels_ref.at[:, z, k, :, pl.ds(lane, LANES)],
                    target.at[:, pl.ds(begin, rows), :],
                    sem.at[z * x_devices + k],
                )
            )
    for copy in copies:
        copy.start()
    return copies


def hidden_kernel(place_ref, got_ref, scale_ref, bias_ref, out_ref, total):
    docs = out_ref.shape[0]
    parts = got_ref.shape[1]

    @pl.loop(0, docs, unroll=4)
    def _(n):
        value = None
        for slot in range(4):
            row = got_ref[place_ref[0, slot * docs + n]].astype(jnp.float32)
            value = row if value is None else value + row
        total[pl.ds(pl.multiple_of(n * parts, parts), parts), :] = value

    scale = scale_ref[...]
    for c in range(parts):
        lanes = slice(c * LANES, (c + 1) * LANES)
        v = total[pl.ds(c, docs, stride=parts), :] * scale + bias_ref[:, lanes]
        soft = jnp.maximum(v, 0.0) + jnp.log1p(jnp.exp(-jnp.abs(v)))
        out_ref[:, lanes] = soft.astype(jnp.bfloat16)


def output_kernel(shift_ref, hidden_ref, noise_ref, panels_ref, bias_ref, out_ref, head, factor, head_sem, factor_sem):
    head_copies = place_panels(shift_ref, panels_ref, 0, head, head_sem)
    factor_copies = place_panels(shift_ref, panels_ref, LANES, factor, factor_sem)
    pieces = head.shape[0]
    width = out_ref.shape[1] // pieces
    for copy in head_copies:
        copy.wait()
    result = bias_ref[...]
    for v in range(0, pieces, 2):
        hidden = hidden_ref[:, v * LANES : (v + 2) * LANES]
        pair = jnp.concatenate([head[v], head[v + 1]], axis=1)
        result = result + lax.dot_general(hidden, pair, NT, preferred_element_type=jnp.float32)
    for copy in factor_copies:
        copy.wait()
    noise = noise_ref[...]
    parts = []
    for v in range(0, pieces, 2):
        pair = jnp.concatenate([factor[v], factor[v + 1]], axis=1)
        both = jnp.dot(noise, pair, preferred_element_type=jnp.float32)
        parts += [both[:, :width], both[:, LANES : LANES + width]]
    out_ref[...] = (result + jnp.concatenate(parts, axis=1)).astype(out_ref.dtype)


def local(
    counts,
    doc_owner,
    doc_sub,
    doc_len,
    first_weight,
    first_bias,
    head_weight,
    head_bias,
    factor,
    noise_draw,
):
    vocab_devices = lax.axis_size("y") * lax.axis_size("core")
    x_devices, z_devices = lax.axis_size("x"), lax.axis_size("z")
    docs_devices = x_devices * z_devices
    devices = vocab_devices * docs_devices
    docs_here, slot_count, block_width = counts.shape
    slots = docs_here * slot_count
    hidden_width = first_weight.shape[1]
    parts = hidden_width // LANES
    topics = noise_draw.shape[1]
    topic_cols = head_weight.shape[1]
    factor_rows = factor.shape[0]

    panel = jnp.concatenate(
        [head_weight.T, jnp.pad(factor.T, ((0, 0), (0, LANES - factor_rows)))], axis=1
    )
    line = [panel]
    for k in range(1, x_devices):
        line.append(lax.ppermute(panel, "x", [((i + k) % x_devices, i) for i in range(x_devices)]))
    rows = counts.transpose(1, 0, 2).reshape(slots, block_width)
    owner_flat = doc_owner.T.reshape(1, slots)
    sub_flat = doc_sub.T.reshape(1, slots)
    send, place = pl.pallas_call(
        route_kernel,
        out_shape=(
            jax.ShapeDtypeStruct((devices * 4, LANES), jnp.bfloat16),
            jax.ShapeDtypeStruct((1, slots), jnp.int32),
        ),
        in_specs=[VMEM] * 3,
        out_specs=(VMEM, VMEM),
        scratch_shapes=[pltpu.VMEM((devices * 4, LANES), jnp.float32)],
        compiler_params=PARAMS,
        cost_estimate=pl.CostEstimate(flops=10**9, bytes_accessed=10**6, transcendentals=0),
    )(owner_flat, sub_flat, rows)
    line, send = lax.optimization_barrier((line, send))
    panels = lax.all_gather(jnp.concatenate(line, axis=0), ("y", "core", "z"), axis=0, tiled=True)
    panels = panels.reshape(vocab_devices, z_devices, x_devices, topic_cols, 2 * LANES)
    shift = lax.axis_index("x").astype(jnp.int32).reshape(1)

    got = lax.all_to_all(
        send.reshape(devices, 4, LANES), AXES, split_axis=0, concat_axis=0, tiled=True
    )
    got = got.reshape(devices * 4, LANES)
    terms = pl.pallas_call(
        owner_kernel,
        out_shape=jax.ShapeDtypeStruct((devices, 2 * parts, LANES), jnp.bfloat16),
        in_specs=[VMEM, pl.BlockSpec(memory_space=pl.ANY)],
        out_specs=VMEM,
        scratch_shapes=[
            pltpu.VMEM((2 * devices, first_weight.shape[0]), jnp.bfloat16),
            pltpu.VMEM((2, devices * 8, LANES), jnp.float32),
            pltpu.VMEM((devices * 4, LANES), jnp.float32),
            pltpu.VMEM(first_weight.shape, jnp.bfloat16),
            pltpu.SemaphoreType.DMA((hidden_width // 256,)),
        ],
        compiler_params=PARAMS,
        cost_estimate=pl.CostEstimate(flops=5 * 10**9, bytes_accessed=10**7, transcendentals=0),
    )(got, first_weight)
    returned = lax.all_to_all(terms, AXES, split_axis=0, concat_axis=0, tiled=True)
    returned = returned.reshape(2 * devices, parts, LANES)

    scale = (128.0 * slot_count / doc_len.astype(jnp.float32))[:, None]
    hidden = pl.pallas_call(
        hidden_kernel,
        out_shape=jax.ShapeDtypeStruct((docs_here, hidden_width), jnp.bfloat16),
        in_specs=[SMEM, VMEM, VMEM, VMEM],
        out_specs=VMEM,
        scratch_shapes=[pltpu.VMEM((docs_here * parts, LANES), jnp.float32)],
        compiler_params=PARAMS,
        cost_estimate=pl.CostEstimate(flops=10**7, bytes_accessed=10**7, transcendentals=10**6),
    )(place, returned, scale, first_bias.reshape(1, hidden_width))
    return pl.pallas_call(
        output_kernel,
        out_shape=jax.ShapeDtypeStruct((docs_here, topics), jnp.bfloat16),
        in_specs=[SMEM, VMEM, VMEM, pl.BlockSpec(memory_space=pl.ANY), VMEM],
        out_specs=VMEM,
        scratch_shapes=[
            pltpu.VMEM((vocab_devices, topics, LANES), jnp.bfloat16),
            pltpu.VMEM((vocab_devices, topics, LANES), jnp.bfloat16),
            pltpu.SemaphoreType.DMA((docs_devices,)),
            pltpu.SemaphoreType.DMA((docs_devices,)),
        ],
        compiler_params=PARAMS,
        cost_estimate=pl.CostEstimate(flops=10**9, bytes_accessed=10**7, transcendentals=0),
    )(shift, hidden, noise_draw, panels, head_bias.reshape(1, topics))


def solution(mesh):
    sizes = (8, 2, 4, 8)
    fine = jax.sharding.Mesh(mesh.devices.reshape(sizes), AXES)
    rows, vocab, docs = P(AXES), ("y", "core"), ("x", "z")
    return jax.shard_map(
        local,
        mesh=fine,
        in_specs=(rows, rows, rows, rows, rows, P(), P(vocab, docs), P(), P(vocab, docs), rows),
        out_specs=rows,
        check_vma=False,
    )
```
